512 devices in a mesh: dp: 512 (over x, y, z, core).
Axes of the slice: x: 4, y: 8, z: 8, core: 2. Of those that a mesh axis runs over, the one named last changes fastest.
Arguments:
- image_emb: bfloat16 [131072, 1152], P('dp'), may hold values from -0.1875 to 0.1875
- text_emb: bfloat16 [131072, 1152], P('dp'), may hold values from -0.1875 to 0.1875
- pair_id: int32 [131072], P('dp'), may hold values from 0 to 32767
- logit_scale: float32 [1], replicated, may hold values from 6 to 14
- logit_bias: float32 [1], replicated, may hold values from -4 to -1
Outputs:
- image_grad: float32 [131072, 1152], P('dp')
- text_grad: float32 [131072, 1152], P('dp')
The draws below stay inside these ranges and needn't reach their ends.
All inputs are finite; a program needn't handle non-finite values.
Results may differ from the reference program's by a relative error of at most 0.0045.
Values may be sent and summed in bfloat16 or wider, within the bound.
A program may use at most 64 MiB of HBM per device.

```python
import jax
import jax.numpy as jnp
from jax import lax

D = 1152
TOK_DEV = 256
ROUNDS = 3
TOKENS = 131072
N_DP = 512


def with_ends(entries, own_key, low, largest):
    longest = entries.shape.index(max(entries.shape))
    spots = []
    for shift in (0, 1):
        where = [jax.random.randint(jax.random.fold_in(own_key, axis), (), 0, length) for axis, length in enumerate(entries.shape)]
        where[longest] = (where[longest] + shift) % entries.shape[longest]
        spots.append(tuple(where))
    return entries.at[spots[0]].set(low).at[spots[1]].set(largest)


def steps_of(key, dims, shards, smallest, largest):
    def one(axis_at, shards_of):
        draws = jax.random.uniform(jax.random.fold_in(jax.random.fold_in(key, 6), axis_at), (shards_of,), jnp.float32, smallest / len(shards), largest / len(shards))
        return jnp.repeat(jnp.exp(draws), dims[axis_at] // shards_of).reshape((-1,) + (1,) * (len(dims) - axis_at - 1))

    factor_of = one(*shards[0])
    for cut in shards[1:]:
        factor_of = factor_of * one(*cut)
    return factor_of


def noise(key, extent, width, bound, split=(), dtype=jnp.bfloat16):
    loudness = steps_of(key, extent, split, -0.22, 0.18) if split else 1.0
    values = jax.random.normal(key, extent, jnp.float32) * width * loudness
    return jnp.minimum(jnp.maximum(values, -bound), bound).astype(dtype)


def setup_inputs(seed: int = 0) -> dict:
    streams_of = jax.random.split(jax.random.key(seed), 6)
    image_emb = noise(streams_of[0], (TOKENS, D), 0.03, 0.1875, ((0, 512),))
    text_emb = noise(streams_of[1], (TOKENS, D), 0.03, 0.1875, ((0, 512),))
    pair_id = with_ends(jax.random.randint(streams_of[2], (TOKENS,), 0, TOKENS // 4), jax.random.fold_in(streams_of[2], 1), 0, (TOKENS // 4) - 1).astype(jnp.int32)
    logit_scale = jnp.clip(jax.random.uniform(streams_of[3], (1,), jnp.float32, 6.0, 14.0), 6.0, 14.0)
    logit_bias = jnp.clip(jax.random.uniform(streams_of[4], (1,), jnp.float32, -4.0, -1.0), -4.0, -1.0)
    return {"image_emb": image_emb, "text_emb": text_emb, "pair_id": pair_id, "logit_scale": logit_scale, "logit_bias": logit_bias}


def normalize(embedding):
    as_float = embedding.astype(jnp.float32)
    row_norms = jnp.sqrt(lax.optimization_barrier(jnp.sum(as_float * as_float, axis=1, keepdims=True)) + 1e-06)
    return (as_float / row_norms, row_norms)

def block_coeff(left_rows, right_rows, left_ids, right_ids, scale_value, bias_value):
    scores = jnp.dot(left_rows, right_rows.T, preferred_element_type=jnp.float32)
    logits = scale_value * scores + bias_value
    positive = (left_ids[:, None] == right_ids[None, :]).astype(jnp.float32)
    return (scale_value * (jax.nn.sigmoid(logits) - positive)).astype(jnp.bfloat16)

def reference(image_emb, text_emb, pair_id, logit_scale, logit_bias):
    scale_value = logit_scale[0]
    bias_value = logit_bias[0]
    unit_img, norm_img = normalize(image_emb)
    unit_txt, norm_txt = normalize(text_emb)
    img_hat = unit_img.astype(jnp.bfloat16)
    txt_hat = unit_txt.astype(jnp.bfloat16)
    offsets = [0]
    for round_index in range(ROUNDS):
        distance = 1 + round_index * (N_DP // 6)
        offsets.append(distance)
        offsets.append(N_DP - distance)
    grad_img = jnp.zeros((N_DP * TOK_DEV, D), jnp.float32)
    grad_txt = jnp.zeros((N_DP * TOK_DEV, D), jnp.float32)
    img_blocks = img_hat.reshape(N_DP, TOK_DEV, D)
    img_ids = pair_id.reshape(N_DP, TOK_DEV)

    def one_block(operands):
        left_rows, right_rows, left_ids, right_ids = operands
        weights = block_coeff(left_rows, right_rows, left_ids, right_ids, scale_value, bias_value)
        left_grad = jnp.dot(weights, right_rows, preferred_element_type=jnp.float32)
        right_grad = jnp.dot(weights.T, left_rows, preferred_element_type=jnp.float32)
        return (left_grad, right_grad)
    for offset in offsets:
        shift_rows = offset * TOK_DEV
        txt_blocks = jnp.roll(txt_hat, -shift_rows, axis=0).reshape(N_DP, TOK_DEV, D)
        txt_ids = jnp.roll(pair_id, -shift_rows, axis=0).reshape(N_DP, TOK_DEV)
        left_grad, right_grad = lax.map(one_block, (img_blocks, txt_blocks, img_ids, txt_ids))
        grad_img = grad_img + left_grad.reshape(N_DP * TOK_DEV, D)
        grad_txt = grad_txt + jnp.roll(right_grad.reshape(N_DP * TOK_DEV, D), shift_rows, axis=0)
    image_grad = (grad_img - unit_img * lax.optimization_barrier(jnp.sum(unit_img * grad_img, axis=1, keepdims=True))) / norm_img
    text_grad = (grad_txt - unit_txt * lax.optimization_barrier(jnp.sum(unit_txt * grad_txt, axis=1, keepdims=True))) / norm_txt
    return (image_grad, text_grad)
```

```python
import jax
import jax.numpy as jnp
from jax import lax
from jax.experimental import pallas as pl
from jax.experimental.pallas import tpu as pltpu
from jax.sharding import PartitionSpec as P

MESH = pl.DeviceIdType.MESH
NDEV = 512
ROWS = 256
D = 1152
CHUNKS = 16
SIZE = 2 * ROWS // CHUNKS
SKEW = 3
HALF = 128
LEGS = ("near", "fix", "fj", "fk", "A", "B", "sk", "sl", "sm", "C", "D")
NEXT = {"near": ("fj", "fix"), "sk": ("sl",), "fj": ("fk",), "sl": ("sm", "D"), "fk": ("A", "B"), "sm": ("C",)}
DELAY = {"near": 0, "sk": 0, "fj": 1, "sl": 1, "fk": 2, "sm": 2, "A": 3, "B": 3, "C": 3, "D": 3}
ORDER = ("A", "B", "C", "D", "fk", "sm", "fj", "sl", "near", "sk")


def coords(i):
    return i // 128, (i // 16) % 8, (i // 2) % 8, i % 2


def index(x, y, z, core):
    return (((x + 8) % 4 * 8 + (y + 16) % 8) * 8 + (z + 16) % 8) * 2 + core


def wrap(i):
    return (i + 2 * NDEV) % NDEV


def side(core):
    return 2 * core - 1


def y_steps(z_start, d):
    return d * 5 + (z_start + 3 * d + 8) // 8 - 1


def along_z(i, n):
    x, y, z, core = coords(i)
    return index(x, y, z + n * side(core), core)


def other_z(i, n):
    x, y, z, core = coords(i)
    return index(x, y, z + n * side(core), 1 - core)


def along_y(i, z_start, d, sign):
    x, y, z, core = coords(i)
    return index(x, y + sign * y_steps(z_start, d), z, core)


def f_z_start(i):
    _, _, z, core = coords(i)
    return (z - 3 * side(core) + 16) % 8


def f_y(i, sign):
    return along_y(i, f_z_start(i), side(i % 2), sign)


def f_hold(owner):
    return f_y(along_z(owner, 3), 1)


def f_owner(i):
    return along_z(f_y(i, -1), -3)


def s_y(i, sign):
    return along_y(i, (i // 2) % 8, -side(i % 2), sign)


def s_hold(owner, n):
    return along_z(s_y(owner, 1), -n)


def s_owner(i, n):
    return s_y(along_z(i, n), -1)


def kernel(scale_ref, bias_ref, ids_ref, img_ref, txt_ref, out_img, out_txt, near, fj, fk, sk, sl, sm, far, part, own,
           hat, keys, coeff, ids, far_ids, send_sem, recv_sem, part_sem, id_sem, own_sem):
    me = lax.axis_index("dp")
    _, _, z, core = coords(me)
    s = side(core)
    barrier = pltpu.get_barrier_semaphore()

    f_own, s_own2, s_own3 = f_owner(me), s_owner(me, 2), s_owner(me, 3)
    target = {
        "near": other_z(me, 1), "fix": wrap(me - 16 * s), "fj": other_z(me, -2), "fk": f_y(me, 1),
        "A": wrap(f_own + 86 * s), "B": wrap(f_own - 171 * s),
        "sk": s_y(me, 1), "sl": along_z(me, -2), "sm": along_z(me, -1),
        "C": wrap(s_own3 - 86 * s), "D": wrap(s_own2 + 171 * s),
    }
    source = {
        "near": other_z(me, 1), "fix": wrap(me + 16 * s), "fj": other_z(me, -2), "fk": f_y(me, -1),
        "A": f_hold(wrap(me - 86 * s)), "B": f_hold(wrap(me - 171 * s)),
        "sk": s_y(me, -1), "sl": along_z(me, 2), "sm": along_z(me, 1),
        "C": s_hold(wrap(me + 86 * s), 3), "D": s_hold(wrap(me + 171 * s), 2),
    }
    partner = wrap(me - s)
    id_to = [partner, wrap(me + s), wrap(me + 86 * s), wrap(me - 171 * s), wrap(me - 86 * s), wrap(me + 171 * s)]
    id_from = [partner, wrap(me + s), wrap(me - 86 * s), wrap(me - 171 * s), wrap(me + 86 * s), wrap(me + 171 * s)]
    only = {"fix": z == 7 * core, "A": target["A"] != me, "C": target["C"] != me}

    own_copies = [pltpu.make_async_copy(r, own.at[a], own_sem.at[a]) for a, r in ((0, img_ref), (1, txt_ref))]
    for copy in own_copies:
        copy.start()

    def signal(device):
        pl.semaphore_signal(barrier, inc=1, device_id=(device,), device_id_type=MESH)

    always = [leg for leg in LEGS if leg not in only]
    for leg in always:
        signal(source[leg])
    for device in id_from:
        signal(device)
    for leg, where in only.items():
        pl.when(where)(lambda leg=leg: signal(source[leg]))
    pl.semaphore_wait(barrier, len(always) + len(id_from) + sum(jnp.where(where, 1, 0) for where in only.values()))

    def own_rows(i):
        first = i * SIZE
        return txt_ref.at[pl.ds(first, SIZE)] if first < ROWS else img_ref.at[pl.ds(first - ROWS, SIZE)]

    def place(leg, i):
        rows = pl.ds(i * SIZE, SIZE)
        if leg in ("near", "fix"):
            return near.at[int(leg == "fix"), rows]
        if leg in "ABCD":
            per = HALF // SIZE
            return far.at[i // per, pl.ds("ABCD".index(leg) * HALF + i % per * SIZE, SIZE)]
        return {"fj": fj, "fk": fk, "sk": sk, "sl": sl, "sm": sm}[leg].at[rows]

    came_by = {out: leg for leg, outs in NEXT.items() for out in outs}

    def start_of(leg, i):
        return place(came_by[leg], i) if leg in came_by else own_rows(i)

    def remote(leg, i):
        j = LEGS.index(leg)
        return pltpu.make_async_remote_copy(
            src_ref=start_of(leg, i), dst_ref=place(leg, i), send_sem=send_sem.at[j, i], recv_sem=recv_sem.at[j, i],
            device_id=(target[leg],), device_id_type=MESH)

    def send(leg, i):
        if leg in only:
            pl.when(only[leg])(lambda: remote(leg, i).start())
            if leg != "fix":
                pl.when(jnp.logical_not(only[leg]))(lambda: pltpu.make_async_copy(
                    start_of(leg, i), place(leg, i), recv_sem.at[LEGS.index(leg), i]).start())
        else:
            remote(leg, i).start()

    def whole(a):
        ref = (txt_ref, img_ref)[a]
        return pltpu.make_async_remote_copy(
            src_ref=ref, dst_ref=part.at[pl.ds(a * ROWS, ROWS)], send_sem=part_sem.at[a], recv_sem=part_sem.at[2 + a],
            device_id=(partner,), device_id_type=MESH)

    def send_ids(j):
        return pltpu.make_async_remote_copy(
            src_ref=ids, dst_ref=far_ids.at[j], send_sem=id_sem.at[j], recv_sem=id_sem.at[6 + j],
            device_id=(id_to[j],), device_id_type=MESH)

    for i in range(CHUNKS):
        send("near", i)
        send("sk", i)
    ids[...] = jnp.broadcast_to(ids_ref[...], (8, ROWS))
    for j in range(6):
        send_ids(j).start()
    for a in range(2):
        whole(a).start()

    scale, bias = scale_ref[0], bias_ref[0]
    diagonal = lax.broadcasted_iota(jnp.int32, (ROWS, ROWS), 0) == lax.broadcasted_iota(jnp.int32, (ROWS, ROWS), 1)
    my_ids = jnp.sum(jnp.where(diagonal, jnp.broadcast_to(ids_ref[...], (ROWS, ROWS)), 0), axis=1, keepdims=True)

    def normalize(read, write, rows):
        def body(i, carry):
            first = pl.multiple_of(i * 32, 32)
            values = read(first).astype(jnp.float32)
            norms = jnp.sqrt(jnp.sum(values * values, axis=1, keepdims=True) + 1e-6)
            write(first, (values * (1.0 / norms)).astype(jnp.bfloat16))
            return carry
        lax.fori_loop(0, rows // 32, body, 0)

    def gain(a, key_rows, key_ids, out, first=False):
        count = key_rows.shape[0]
        scores = lax.dot_general(hat[a], key_rows[...], (((1,), (1,)), ((), ())), preferred_element_type=jnp.float32)
        positive = (my_ids == key_ids).astype(jnp.float32)
        coeff[:, pl.ds(0, count)] = (scale * (jax.nn.sigmoid(scale * scores + bias) - positive)).astype(jnp.bfloat16)
        term = jnp.dot(coeff[:, pl.ds(0, count)], key_rows[...], preferred_element_type=jnp.float32)
        if first:
            out[...] = term
        else:
            out[...] += term

    def keys_from(read, rows):
        def write(first, value):
            keys[pl.ds(first, 32)] = value
        normalize(read, write, rows)
        return keys.at[pl.ds(0, rows)]

    outs = (out_img, out_txt)

    def own_step():
        for a in range(2):
            own_copies[a].wait()
            def write(first, value):
                hat[a, pl.ds(first, 32)] = value
            normalize(lambda first: own[a, pl.ds(first, 32)], write, ROWS)
        for a in range(2):
            gain(a, hat.at[1 - a], ids_ref[...], outs[a], first=True)

    def partner_step(a):
        whole(a).wait_recv()
        rows = keys_from(lambda first: part[pl.ds(a * ROWS + first, 32)], ROWS)
        gain(a, rows, far_ids[0, pl.ds(0, 1)], outs[a])

    def near_step(a):
        for i in range(a * CHUNKS // 2, (a + 1) * CHUNKS // 2):
            pl.when(only["fix"])(lambda: remote("fix", i).wait_recv())
        slot = jnp.where(only["fix"], 1, 0)
        rows = keys_from(lambda first: near[slot, pl.ds(a * ROWS + first, 32)], ROWS)
        gain(a, rows, far_ids[1, pl.ds(0, 1)], outs[a])

    def far_step(part_of):
        a, half = part_of // 2, part_of % 2
        rows = keys_from(lambda first: far[part_of, pl.ds(first, 32)], 4 * HALF)
        lanes = pl.ds(half * HALF, HALF)
        key_ids = jnp.concatenate([far_ids[j, pl.ds(0, 1), lanes] for j in range(2, 6)], axis=1)
        gain(a, rows, key_ids, outs[a])

    todo = {1: own_step, 2: lambda: [send_ids(j).wait_recv() for j in range(6)] and partner_step(0),
            3: lambda: partner_step(1), 9: lambda: near_step(0), 17: lambda: near_step(1)}
    for t in range(CHUNKS + 3 * SKEW):
        for leg in ORDER:
            i = t - DELAY[leg] * SKEW
            if 0 <= i < CHUNKS:
                remote(leg, i).wait_recv()
                for out in NEXT.get(leg, ()):
                    send(out, i)
        if t in todo:
            todo[t]()
        i = t - 3 * SKEW
        if 0 <= i and (i + 1) % (HALF // SIZE) == 0:
            far_step(i // (HALF // SIZE))

    for a, ref, out in ((0, img_ref, out_img), (1, txt_ref, out_txt)):
        def body(i, carry):
            rows = pl.ds(pl.multiple_of(i * 32, 32), 32)
            values = own[a, rows].astype(jnp.float32)
            inverse = 1.0 / jnp.sqrt(jnp.sum(values * values, axis=1, keepdims=True) + 1e-6)
            unit = values * inverse
            grad = out[rows]
            out[rows] = (grad - unit * jnp.sum(unit * grad, axis=1, keepdims=True)) * inverse
            return carry
        lax.fori_loop(0, ROWS // 32, body, 0)

    for i in range(CHUNKS):
        for leg in LEGS:
            if leg in only:
                pl.when(only[leg])(lambda: remote(leg, i).wait_send())
            else:
                remote(leg, i).wait_send()
    for a in range(2):
        whole(a).wait_send()
    for j in range(6):
        send_ids(j).wait_send()


def per_device(image_emb, text_emb, pair_id, logit_scale, logit_bias):
    def rows(*shape):
        return pltpu.VMEM(shape, jnp.bfloat16)
    smem, vmem = (pl.BlockSpec(memory_space=m) for m in (pltpu.SMEM, pltpu.VMEM))
    grad = jax.ShapeDtypeStruct((ROWS, D), jnp.float32)
    return pl.pallas_call(
        kernel,
        out_shape=(grad, grad),
        in_specs=[smem, smem, vmem, pl.BlockSpec(memory_space=pl.ANY), pl.BlockSpec(memory_space=pl.ANY)],
        out_specs=(vmem, vmem),
        scratch_shapes=[
            rows(2, 2 * ROWS, D), *[rows(2 * ROWS, D)] * 5, rows(4, 4 * HALF, D), rows(2 * ROWS, D), rows(2, ROWS, D),
            rows(2, ROWS, D), rows(4 * HALF, D), rows(ROWS, 4 * HALF),
            pltpu.VMEM((8, ROWS), jnp.int32), pltpu.VMEM((6, 8, ROWS), jnp.int32),
            pltpu.SemaphoreType.DMA((len(LEGS), CHUNKS)), pltpu.SemaphoreType.DMA((len(LEGS), CHUNKS)),
            pltpu.SemaphoreType.DMA((4,)), pltpu.SemaphoreType.DMA((12,)), pltpu.SemaphoreType.DMA((2,)),
        ],
        compiler_params=pltpu.CompilerParams(collective_id=0, has_side_effects=True, vmem_limit_bytes=48 * 2**20),
        cost_estimate=pl.CostEstimate(flops=28 * ROWS * ROWS * D * 2, bytes_accessed=6 * ROWS * D * 4, transcendentals=14 * ROWS * ROWS),
    )(logit_scale, logit_bias, pair_id.reshape(1, ROWS), image_emb, text_emb)


def solution(mesh):
    in_specs = (P("dp", None), P("dp", None), P("dp"), P(), P())
    out_specs = (P("dp", None), P("dp", None))
    return jax.shard_map(
        per_device, mesh=mesh, in_specs=in_specs, out_specs=out_specs, check_vma=False
    )
```

```python
import jax
import jax.numpy as jnp
from jax import lax
from jax.experimental import pallas as pl
from jax.experimental.pallas import tpu as pltpu
from jax.sharding import PartitionSpec as P

MESH = pl.DeviceIdType.MESH
NDEV = 512
ROWS = 256
D = 1152
CHUNKS = 16
SIZE = 2 * ROWS // CHUNKS
HALF = 128
NORM_ROWS = 64
PROJECT_ROWS = 64
VMEM_LIMIT = 56 * 2**20
LEGS = ("near", "fix", "fj", "fk", "A", "B", "sk", "sl", "sm", "C", "D")
NEXT = {"near": ("fj", "fix"), "sk": ("sl",), "fj": ("fk",), "sl": ("sm", "D"), "fk": ("A", "B"), "sm": ("C",)}
DELAY = {"near": 0, "sk": 0, "fj": 3, "sl": 3, "fk": 6, "sm": 6, "A": 9, "B": 9, "C": 9, "D": 9}
ORDER = ("A", "B", "C", "D", "fk", "sm", "fj", "sl", "near", "sk")
CLOSE_AT = (10, 18)


def coords(i):
    return i // 128, (i // 16) % 8, (i // 2) % 8, i % 2


def index(x, y, z, core):
    return (((x + 8) % 4 * 8 + (y + 16) % 8) * 8 + (z + 16) % 8) * 2 + core


def wrap(i):
    return (i + 2 * NDEV) % NDEV


def side(core):
    return 2 * core - 1


def y_steps(z_start, d):
    return d * 5 + (z_start + 3 * d + 8) // 8 - 1


def along_z(i, n):
    x, y, z, core = coords(i)
    return index(x, y, z + n * side(core), core)


def other_z(i, n):
    x, y, z, core = coords(i)
    return index(x, y, z + n * side(core), 1 - core)


def along_y(i, z_start, d, sign):
    x, y, z, core = coords(i)
    return index(x, y + sign * y_steps(z_start, d), z, core)


def f_z_start(i):
    _, _, z, core = coords(i)
    return (z - 3 * side(core) + 16) % 8


def f_y(i, sign):
    return along_y(i, f_z_start(i), side(i % 2), sign)


def f_hold(owner):
    return f_y(along_z(owner, 3), 1)


def f_owner(i):
    return along_z(f_y(i, -1), -3)


def s_y(i, sign):
    return along_y(i, (i // 2) % 8, -side(i % 2), sign)


def s_hold(owner, n):
    return along_z(s_y(owner, 1), -n)


def s_owner(i, n):
    return s_y(along_z(i, n), -1)


def kernel(scale_ref, bias_ref, ids_ref, img_ref, txt_ref, out_img, out_txt, close, fj, sk, sl, far, raw, coeff, ids,
           far_ids, send_sem, recv_sem, part_sem, id_sem, own_sem):
    me = lax.axis_index("dp")
    _, _, z, core = coords(me)
    s = side(core)
    barrier = pltpu.get_barrier_semaphore()

    own_copies = [pltpu.make_async_copy(r, raw.at[a], own_sem.at[a]) for a, r in ((0, txt_ref), (1, img_ref))]
    for copy in own_copies:
        copy.start()

    def is_edge(z, core):
        return z == 7 * core

    f_own, s_own2, s_own3 = f_owner(me), s_owner(me, 2), s_owner(me, 3)
    target = {
        "near": other_z(me, 1), "fix": wrap(me - 16 * s), "fj": other_z(me, -2), "fk": f_y(me, 1),
        "A": wrap(f_own + 86 * s), "B": wrap(f_own - 171 * s),
        "sk": s_y(me, 1), "sl": along_z(me, -2), "sm": along_z(me, -1),
        "C": wrap(s_own3 - 86 * s), "D": wrap(s_own2 + 171 * s),
    }
    source = {
        "near": other_z(me, 1), "fix": wrap(me + 16 * s), "fj": other_z(me, -2), "fk": f_y(me, -1),
        "A": f_hold(wrap(me - 86 * s)), "B": f_hold(wrap(me - 171 * s)),
        "sk": s_y(me, -1), "sl": along_z(me, 2), "sm": along_z(me, 1),
        "C": s_hold(wrap(me + 86 * s), 3), "D": s_hold(wrap(me + 171 * s), 2),
    }
    partner = wrap(me - s)
    id_to = [partner, wrap(me + s), wrap(me + 86 * s), wrap(me - 171 * s), wrap(me - 86 * s), wrap(me + 171 * s)]
    id_from = [partner, wrap(me + s), wrap(me - 86 * s), wrap(me - 171 * s), wrap(me + 86 * s), wrap(me + 171 * s)]
    only = {"fix": is_edge(z, core), "A": target["A"] != me, "C": target["C"] != me}
    passes = {leg: jnp.where(where, 1, 0) for leg, where in only.items()}

    def signal(device):
        pl.semaphore_signal(barrier, inc=1, device_id=(device,), device_id_type=MESH)

    always = [leg for leg in LEGS if leg not in only]
    for leg in always:
        signal(source[leg])
    for device in id_from:
        signal(device)
    for leg, where in only.items():
        pl.when(where)(lambda leg=leg: signal(source[leg]))

    for a in range(2):
        own_copies[a].wait()

        def body(i, carry):
            first = pl.multiple_of(i * NORM_ROWS, NORM_ROWS)
            values = raw[a, pl.ds(first, NORM_ROWS)].astype(jnp.float32)
            norms = jnp.sqrt(jnp.sum(values * values, axis=1, keepdims=True) + 1e-6)
            close[0, pl.ds(a * ROWS + first, NORM_ROWS)] = (values * (1.0 / norms)).astype(jnp.bfloat16)
            return carry
        lax.fori_loop(0, ROWS // NORM_ROWS, body, 0)
    ids[...] = jnp.broadcast_to(ids_ref[...], (8, ROWS))

    pl.semaphore_wait(barrier, len(always) + len(id_from) + sum(passes.values()))

    _, _, next_z, next_core = coords(target["near"])
    near_slot = 2 + passes["fix"]
    near_slot_there = 2 + jnp.where(is_edge(next_z, next_core), 1, 0)
    f_next, s_next = target["fk"], target["sm"]
    a_there = jnp.where(wrap(f_owner(f_next) + 86 * s) != f_next, 4, 0)
    c_there = jnp.where(wrap(s_owner(s_next, 3) - 86 * s) != s_next, 5, 2)
    a_here, c_here = 4 * passes["A"], 2 + 3 * passes["C"]

    def far_rows(slot, i):
        per = HALF // SIZE
        return far.at[i // per, pl.ds(pl.multiple_of(slot * HALF + i % per * SIZE, SIZE), SIZE)]

    def to(leg, i):
        rows = pl.ds(i * SIZE, SIZE)
        if leg == "near":
            return close.at[near_slot_there, rows]
        if leg == "fix":
            return close.at[2, rows]
        if leg == "fk":
            return far_rows(a_there, i)
        if leg == "sm":
            return far_rows(c_there, i)
        if leg in "ABCD":
            return far_rows("ABCD".index(leg), i)
        return {"fj": fj, "sk": sk, "sl": sl}[leg].at[rows]

    def at(leg, i):
        if leg == "near":
            return close.at[near_slot, pl.ds(i * SIZE, SIZE)]
        if leg == "fk":
            return far_rows(a_here, i)
        if leg == "sm":
            return far_rows(c_here, i)
        return to(leg, i)

    came_by = {out: leg for leg, outs in NEXT.items() for out in outs}

    def remote(leg, i):
        j = LEGS.index(leg)
        return pltpu.make_async_remote_copy(
            src_ref=at(came_by[leg], i) if leg in came_by else close.at[0, pl.ds(i * SIZE, SIZE)],
            dst_ref=to(leg, i), send_sem=send_sem.at[j, i], recv_sem=recv_sem.at[j, i],
            device_id=(target[leg],), device_id_type=MESH)

    def do(leg, i, what):
        if leg in only:
            pl.when(only[leg])(lambda: getattr(remote(leg, i), what)())
        else:
            getattr(remote(leg, i), what)()

    def whole():
        return pltpu.make_async_remote_copy(
            src_ref=close.at[0], dst_ref=close.at[1], send_sem=part_sem.at[0], recv_sem=part_sem.at[1],
            device_id=(partner,), device_id_type=MESH)

    def send_ids(j):
        return pltpu.make_async_remote_copy(
            src_ref=ids, dst_ref=far_ids.at[j], send_sem=id_sem.at[j], recv_sem=id_sem.at[6 + j],
            device_id=(id_to[j],), device_id_type=MESH)

    for i in range(CHUNKS):
        do("near", i, "start")
        do("sk", i, "start")
    for j in range(6):
        send_ids(j).start()
    whole().start()

    scale, bias = scale_ref[0], bias_ref[0]
    diagonal = lax.broadcasted_iota(jnp.int32, (ROWS, ROWS), 0) == lax.broadcasted_iota(jnp.int32, (ROWS, ROWS), 1)
    my_ids = jnp.sum(jnp.where(diagonal, jnp.broadcast_to(ids_ref[...], (ROWS, ROWS)), 0), axis=1, keepdims=True)

    outs = (out_img, out_txt)

    def gain(a, key_rows, key_ids, first=False):
        scores = lax.dot_general(close[0, pl.ds((1 - a) * ROWS, ROWS)], key_rows, (((1,), (1,)), ((), ())),
                                 preferred_element_type=jnp.float32)
        positive = (my_ids == key_ids).astype(jnp.float32)
        count = key_rows.shape[0]
        coeff[:, pl.ds(0, count)] = (scale * (jax.nn.sigmoid(scale * scores + bias) - positive)).astype(jnp.bfloat16)
        term = jnp.dot(coeff[:, pl.ds(0, count)], key_rows, preferred_element_type=jnp.float32)
        if first:
            outs[a][...] = term
        else:
            outs[a][...] += term

    def close_step(a):
        if a == 0:
            whole().wait_recv()
            for j in range(6):
                send_ids(j).wait_recv()
        for i in range(a * CHUNKS // 2, (a + 1) * CHUNKS // 2):
            do("fix", i, "wait_recv")
        key_ids = jnp.concatenate([ids_ref[...], far_ids[0, pl.ds(0, 1)], far_ids[1, pl.ds(0, 1)]], axis=1)
        gain(a, close[pl.ds(0, 3), pl.ds(a * ROWS, ROWS)].reshape(3 * ROWS, D), key_ids, first=True)

    def far_step(part_of):
        a, half = part_of // 2, part_of % 2
        lanes = pl.ds(half * HALF, HALF)
        key_ids = jnp.concatenate([far_ids[j, pl.ds(0, 1), lanes] for j in range(2, 6)], axis=1)
        gain(a, far[part_of, pl.ds(0, 4 * HALF)], key_ids)

    for t in range(CHUNKS + max(DELAY.values())):
        for leg in ORDER:
            i = t - DELAY[leg]
            if 0 <= i < CHUNKS:
                do(leg, i, "wait_recv")
                for out in NEXT.get(leg, ()):
                    do(out, i, "start")
        if t in CLOSE_AT:
            close_step(CLOSE_AT.index(t))
        i = t - max(DELAY.values())
        if 0 <= i < CHUNKS - 1:
            for leg in LEGS:
                do(leg, i, "wait_send")
        if 0 <= i and (i + 1) % (HALF // SIZE) == 0:
            far_step(i // (HALF // SIZE))

    for leg in LEGS:
        do(leg, CHUNKS - 1, "wait_send")
    whole().wait_send()
    for j in range(6):
        send_ids(j).wait_send()


def project(grad_img, grad_txt, img, txt, out_img, out_txt, grads, raw, result, sem):
    pieces = [(a, pl.ds(i * PROJECT_ROWS, PROJECT_ROWS), i) for i in range(ROWS // PROJECT_ROWS) for a in range(2)]

    refs = ((grad_img, img, out_img), (grad_txt, txt, out_txt))

    def load_grad(a, rows, i):
        return pltpu.make_async_copy(refs[a][0].at[rows], grads.at[a, rows], sem.at[0, a, i])

    def load_emb(a, rows, i):
        return pltpu.make_async_copy(refs[a][1].at[rows], raw.at[a, rows], sem.at[1, a, i])

    def store(a, rows, i):
        return pltpu.make_async_copy(result.at[a, rows], refs[a][2].at[rows], sem.at[2, a, i])

    for piece in pieces:
        load_grad(*piece).start()
        load_emb(*piece).start()
    for a, rows, i in pieces:
        load_grad(a, rows, i).wait()
        load_emb(a, rows, i).wait()
        values, grad = raw[a, rows].astype(jnp.float32), grads[a, rows]
        inverse = 1.0 / jnp.sqrt(jnp.sum(values * values, axis=1, keepdims=True) + 1e-6)
        along = jnp.sum(values * grad, axis=1, keepdims=True) * (inverse * inverse)
        result[a, rows] = (grad - values * along) * inverse
        store(a, rows, i).start()
    for piece in pieces:
        store(*piece).wait()


def per_device(image_emb, text_emb, pair_id, logit_scale, logit_bias):
    def rows(*shape):
        return pltpu.VMEM(shape, jnp.bfloat16)
    smem, vmem = (pl.BlockSpec(memory_space=m) for m in (pltpu.SMEM, pltpu.VMEM))
    hbm = pl.BlockSpec(memory_space=pltpu.HBM)
    grad = jax.ShapeDtypeStruct((ROWS, D), jnp.float32)
    sums = pl.pallas_call(
        kernel,
        out_shape=(grad, grad),
        in_specs=[smem, smem, vmem, hbm, hbm],
        out_specs=(vmem, vmem),
        scratch_shapes=[
            rows(4, 2 * ROWS, D), *[rows(2 * ROWS, D)] * 3, rows(4, 6 * HALF, D), rows(2, ROWS, D), rows(ROWS, 3 * ROWS),
            pltpu.VMEM((8, ROWS), jnp.int32), pltpu.VMEM((6, 8, ROWS), jnp.int32),
            pltpu.SemaphoreType.DMA((len(LEGS), CHUNKS)), pltpu.SemaphoreType.DMA((len(LEGS), CHUNKS)),
            pltpu.SemaphoreType.DMA((2,)), pltpu.SemaphoreType.DMA((12,)), pltpu.SemaphoreType.DMA((2,)),
        ],
        compiler_params=pltpu.CompilerParams(collective_id=0, has_side_effects=True, vmem_limit_bytes=VMEM_LIMIT),
        cost_estimate=pl.CostEstimate(flops=28 * ROWS * ROWS * D * 2, bytes_accessed=6 * ROWS * D * 4, transcendentals=14 * ROWS * ROWS),
    )(logit_scale, logit_bias, pair_id.reshape(1, ROWS), image_emb, text_emb)
    return pl.pallas_call(
        project, out_shape=(grad, grad), in_specs=[hbm] * 4, out_specs=(hbm, hbm),
        scratch_shapes=[pltpu.VMEM((2, ROWS, D), jnp.float32), rows(2, ROWS, D), pltpu.VMEM((2, ROWS, D), jnp.float32),
                        pltpu.SemaphoreType.DMA((3, 2, ROWS // PROJECT_ROWS))],
        compiler_params=pltpu.CompilerParams(vmem_limit_bytes=VMEM_LIMIT),
        cost_estimate=pl.CostEstimate(flops=16 * ROWS * D, bytes_accessed=20 * ROWS * D, transcendentals=0),
    )(*sums, image_emb, text_emb)


def solution(mesh):
    in_specs = (P("dp", None), P("dp", None), P("dp"), P(), P())
    out_specs = (P("dp", None), P("dp", None))
    return jax.shard_map(
        per_device, mesh=mesh, in_specs=in_specs, out_specs=out_specs, check_vma=False
    )
```

```python
import jax
import jax.numpy as jnp
from jax import lax
from jax.experimental import pallas as pl
from jax.experimental.pallas import tpu as pltpu
from jax.sharding import PartitionSpec as P

MESH = pl.DeviceIdType.MESH
NDEV = 512
ROWS = 256
D = 1152
CHUNKS = 16
SIZE = 2 * ROWS // CHUNKS
HALF = 128
NORM_ROWS = 64
PROJECT_ROWS = 64
VMEM_LIMIT = 56 * 2**20
LEGS = ("near", "fix", "fj", "fk", "A", "B", "sk", "sl", "sm", "C", "D", "part")
NEXT = {"near": ("fj", "fix"), "sk": ("sl",), "fj": ("fk",), "sl": ("sm", "D"), "fk": ("A", "B"), "sm": ("C",)}
DELAY = {"near": 0, "sk": 0, "fj": 3, "sl": 3, "fk": 6, "sm": 6, "A": 9, "B": 9, "C": 9, "D": 9}
ORDER = ("A", "B", "C", "D", "fk", "sm", "fj", "sl", "near", "sk")
PART_AT = 0
WORK = {16: ("image", 0), 17: ("far", 0), 19: ("text", 1), 20: ("far", 1), 22: ("far", 2)}


def coords(i):
    return i // 128, (i // 16) % 8, (i // 2) % 8, i % 2


def index(x, y, z, core):
    return (((x + 8) % 4 * 8 + (y + 16) % 8) * 8 + (z + 16) % 8) * 2 + core


def wrap(i):
    return (i + 2 * NDEV) % NDEV


def side(core):
    return 2 * core - 1


def y_steps(z_start, d):
    return d * 5 + (z_start + 3 * d + 8) // 8 - 1


def along_z(i, n):
    x, y, z, core = coords(i)
    return index(x, y, z + n * side(core), core)


def other_z(i, n):
    x, y, z, core = coords(i)
    return index(x, y, z + n * side(core), 1 - core)


def along_y(i, z_start, d, sign):
    x, y, z, core = coords(i)
    return index(x, y + sign * y_steps(z_start, d), z, core)


def f_z_start(i):
    _, _, z, core = coords(i)
    return (z - 3 * side(core) + 16) % 8


def f_y(i, sign):
    return along_y(i, f_z_start(i), side(i % 2), sign)


def f_hold(owner):
    return f_y(along_z(owner, 3), 1)


def f_owner(i):
    return along_z(f_y(i, -1), -3)


def s_y(i, sign):
    return along_y(i, (i // 2) % 8, -side(i % 2), sign)


def s_hold(owner, n):
    return along_z(s_y(owner, 1), -n)


def s_owner(i, n):
    return s_y(along_z(i, n), -1)


def kernel(scale_ref, bias_ref, ids_ref, img_ref, txt_ref, out_img, out_txt, close, fj, sk, sl, far, raw, coeff, ids,
           far_ids, send_sem, recv_sem, id_sem, own_sem):
    me = lax.axis_index("dp")
    _, _, z, core = coords(me)
    s = side(core)
    barrier = pltpu.get_barrier_semaphore()

    own_copies = [pltpu.make_async_copy(r, raw.at[a], own_sem.at[a]) for a, r in ((0, txt_ref), (1, img_ref))]
    for copy in own_copies:
        copy.start()

    def is_edge(z, core):
        return z == 7 * core

    f_own, s_own2, s_own3 = f_owner(me), s_owner(me, 2), s_owner(me, 3)
    target = {
        "near": other_z(me, 1), "fix": wrap(me - 16 * s), "fj": other_z(me, -2), "fk": f_y(me, 1),
        "A": wrap(f_own + 86 * s), "B": wrap(f_own - 171 * s),
        "sk": s_y(me, 1), "sl": along_z(me, -2), "sm": along_z(me, -1),
        "C": wrap(s_own3 - 86 * s), "D": wrap(s_own2 + 171 * s), "part": wrap(me - s),
    }
    source = {
        "near": other_z(me, 1), "fix": wrap(me + 16 * s), "fj": other_z(me, -2), "fk": f_y(me, -1),
        "A": f_hold(wrap(me - 86 * s)), "B": f_hold(wrap(me - 171 * s)),
        "sk": s_y(me, -1), "sl": along_z(me, 2), "sm": along_z(me, 1),
        "C": s_hold(wrap(me + 86 * s), 3), "D": s_hold(wrap(me + 171 * s), 2), "part": wrap(me - s),
    }
    partner = target["part"]
    id_to = [partner, wrap(me + s), wrap(me + 86 * s), wrap(me - 171 * s), wrap(me - 86 * s), wrap(me + 171 * s)]
    id_from = [partner, wrap(me + s), wrap(me - 86 * s), wrap(me - 171 * s), wrap(me + 86 * s), wrap(me + 171 * s)]
    only = {"fix": is_edge(z, core), "A": target["A"] != me, "C": target["C"] != me}
    passes = {leg: jnp.where(where, 1, 0) for leg, where in only.items()}

    def signal(device):
        pl.semaphore_signal(barrier, inc=1, device_id=(device,), device_id_type=MESH)

    always = [leg for leg in LEGS if leg not in only]
    for leg in always:
        signal(source[leg])
    for device in id_from:
        signal(device)
    for leg, where in only.items():
        pl.when(where)(lambda leg=leg: signal(source[leg]))

    for a in range(2):
        own_copies[a].wait()

        def body(i, carry):
            first = pl.multiple_of(i * NORM_ROWS, NORM_ROWS)
            values = raw[a, pl.ds(first, NORM_ROWS)].astype(jnp.float32)
            norms = jnp.sqrt(jnp.sum(values * values, axis=1, keepdims=True) + 1e-6)
            close[0, pl.ds(a * ROWS + first, NORM_ROWS)] = (values * (1.0 / norms)).astype(jnp.bfloat16)
            return carry
        lax.fori_loop(0, ROWS // NORM_ROWS, body, 0)
    ids[...] = jnp.broadcast_to(ids_ref[...], (8, ROWS))

    pl.semaphore_wait(barrier, len(always) + len(id_from) + sum(passes.values()))

    _, _, next_z, next_core = coords(target["near"])
    near_slot = 2 + passes["fix"]
    near_slot_there = 2 + jnp.where(is_edge(next_z, next_core), 1, 0)
    f_next, s_next = target["fk"], target["sm"]
    a_there = jnp.where(wrap(f_owner(f_next) + 86 * s) != f_next, 4, 0)
    c_there = jnp.where(wrap(s_owner(s_next, 3) - 86 * s) != s_next, 5, 2)
    a_here, c_here = 4 * passes["A"], 2 + 3 * passes["C"]

    def far_rows(slot, i):
        per = HALF // SIZE
        return far.at[i // per, pl.ds(pl.multiple_of(slot * HALF + i % per * SIZE, SIZE), SIZE)]

    def to(leg, i):
        rows = pl.ds(i * SIZE, SIZE)
        if leg == "near":
            return close.at[near_slot_there, rows]
        if leg == "fix":
            return close.at[2, rows]
        if leg == "part":
            return close.at[1, rows]
        if leg == "fk":
            return far_rows(a_there, i)
        if leg == "sm":
            return far_rows(c_there, i)
        if leg in "ABCD":
            return far_rows("ABCD".index(leg), i)
        return {"fj": fj, "sk": sk, "sl": sl}[leg].at[rows]

    def at(leg, i):
        if leg == "near":
            return close.at[near_slot, pl.ds(i * SIZE, SIZE)]
        if leg == "fk":
            return far_rows(a_here, i)
        if leg == "sm":
            return far_rows(c_here, i)
        return to(leg, i)

    came_by = {out: leg for leg, outs in NEXT.items() for out in outs}

    def remote(leg, i):
        j = LEGS.index(leg)
        return pltpu.make_async_remote_copy(
            src_ref=at(came_by[leg], i) if leg in came_by else close.at[0, pl.ds(i * SIZE, SIZE)],
            dst_ref=to(leg, i), send_sem=send_sem.at[j, i], recv_sem=recv_sem.at[j, i],
            device_id=(target[leg],), device_id_type=MESH)

    def do(leg, i, what):
        if leg in only:
            pl.when(only[leg])(lambda: getattr(remote(leg, i), what)())
        else:
            getattr(remote(leg, i), what)()

    def send_ids(j):
        return pltpu.make_async_remote_copy(
            src_ref=ids, dst_ref=far_ids.at[j], send_sem=id_sem.at[j], recv_sem=id_sem.at[6 + j],
            device_id=(id_to[j],), device_id_type=MESH)

    for i in range(CHUNKS):
        do("near", i, "start")
        do("sk", i, "start")
    for j in range(6):
        send_ids(j).start()

    scale, bias = scale_ref[0], bias_ref[0]
    diagonal = lax.broadcasted_iota(jnp.int32, (ROWS, ROWS), 0) == lax.broadcasted_iota(jnp.int32, (ROWS, ROWS), 1)
    my_ids = jnp.sum(jnp.where(diagonal, jnp.broadcast_to(ids_ref[...], (ROWS, ROWS)), 0), axis=1, keepdims=True)

    outs = (out_img, out_txt)

    def gain(a, key_rows, key_ids, first=False):
        count = key_rows.shape[0]
        scores = lax.dot_general(close[0, pl.ds((1 - a) * ROWS, ROWS)], key_rows, (((1,), (1,)), ((), ())),
                                 preferred_element_type=jnp.float32)
        positive = (my_ids == key_ids).astype(jnp.float32)
        coeff[:, pl.ds(0, count)] = (scale * (jax.nn.sigmoid(scale * scores + bias) - positive)).astype(jnp.bfloat16)
        term = jnp.dot(coeff[:, pl.ds(0, count)], key_rows, preferred_element_type=jnp.float32)
        if first:
            outs[a][...] = term
        else:
            outs[a][...] += term

    def close_step(a):
        if a == 0:
            for j in range(6):
                send_ids(j).wait_recv()
        for i in range(a * CHUNKS // 2, (a + 1) * CHUNKS // 2):
            do("fix", i, "wait_recv")
            do("part", i, "wait_recv")
        key_ids = jnp.concatenate([ids_ref[...], far_ids[0, pl.ds(0, 1)], far_ids[1, pl.ds(0, 1)]], axis=1)
        gain(a, close[pl.ds(0, 3), pl.ds(a * ROWS, ROWS)].reshape(3 * ROWS, D), key_ids, first=True)

    def far_step(part_of):
        a, half = part_of // 2, part_of % 2
        lanes = pl.ds(half * HALF, HALF)
        key_ids = jnp.concatenate([far_ids[j, pl.ds(0, 1), lanes] for j in range(2, 6)], axis=1)
        gain(a, far[part_of, pl.ds(0, 4 * HALF)], key_ids)

    last = max(DELAY.values())
    for t in range(CHUNKS + last):
        for leg in ORDER:
            i = t - DELAY[leg]
            if 0 <= i < CHUNKS:
                do(leg, i, "wait_recv")
                for out in NEXT.get(leg, ()):
                    do(out, i, "start")
        if 0 <= t - PART_AT < CHUNKS:
            do("part", t - PART_AT, "start")
        if t in WORK:
            kind, which = WORK[t]
            far_step(which) if kind == "far" else close_step(which)
        if 0 <= t - last < CHUNKS - 1:
            for leg in LEGS:
                do(leg, t - last, "wait_send")
    far_step(3)

    for leg in LEGS:
        do(leg, CHUNKS - 1, "wait_send")
    for j in range(6):
        send_ids(j).wait_send()


def project(grad_img, grad_txt, img, txt, out_img, out_txt, grads, raw, result, sem):
    pieces = [(a, pl.ds(i * PROJECT_ROWS, PROJECT_ROWS), i) for i in range(ROWS // PROJECT_ROWS) for a in range(2)]

    refs = ((grad_img, img, out_img), (grad_txt, txt, out_txt))

    def load_grad(a, rows, i):
        return pltpu.make_async_copy(refs[a][0].at[rows], grads.at[a, rows], sem.at[0, a, i])

    def load_emb(a, rows, i):
        return pltpu.make_async_copy(refs[a][1].at[rows], raw.at[a, rows], sem.at[1, a, i])

    def store(a, rows, i):
        return pltpu.make_async_copy(result.at[a, rows], refs[a][2].at[rows], sem.at[2, a, i])

    for piece in pieces:
        load_grad(*piece).start()
        load_emb(*piece).start()
    for a, rows, i in pieces:
        load_grad(a, rows, i).wait()
        load_emb(a, rows, i).wait()
        values, grad = raw[a, rows].astype(jnp.float32), grads[a, rows]
        inverse = 1.0 / jnp.sqrt(jnp.sum(values * values, axis=1, keepdims=True) + 1e-6)
        along = jnp.sum(values * grad, axis=1, keepdims=True) * (inverse * inverse)
        result[a, rows] = (grad - values * along) * inverse
        store(a, rows, i).start()
    for piece in pieces:
        store(*piece).wait()


def per_device(image_emb, text_emb, pair_id, logit_scale, logit_bias):
    def rows(*shape):
        return pltpu.VMEM(shape, jnp.bfloat16)
    smem, vmem = (pl.BlockSpec(memory_space=m) for m in (pltpu.SMEM, pltpu.VMEM))
    hbm = pl.BlockSpec(memory_space=pltpu.HBM)
    grad = jax.ShapeDtypeStruct((ROWS, D), jnp.float32)
    sums = pl.pallas_call(
        kernel,
        out_shape=(grad, grad),
        in_specs=[smem, smem, vmem, hbm, hbm],
        out_specs=(vmem, vmem),
        scratch_shapes=[
            rows(4, 2 * ROWS, D), *[rows(2 * ROWS, D)] * 3, rows(4, 6 * HALF, D), rows(2, ROWS, D), rows(ROWS, 3 * ROWS),
            pltpu.VMEM((8, ROWS), jnp.int32), pltpu.VMEM((6, 8, ROWS), jnp.int32),
            pltpu.SemaphoreType.DMA((len(LEGS), CHUNKS)), pltpu.SemaphoreType.DMA((len(LEGS), CHUNKS)),
            pltpu.SemaphoreType.DMA((12,)), pltpu.SemaphoreType.DMA((2,)),
        ],
        compiler_params=pltpu.CompilerParams(collective_id=0, has_side_effects=True, vmem_limit_bytes=VMEM_LIMIT),
        cost_estimate=pl.CostEstimate(flops=28 * ROWS * ROWS * D * 2, bytes_accessed=6 * ROWS * D * 4, transcendentals=14 * ROWS * ROWS),
    )(logit_scale, logit_bias, pair_id.reshape(1, ROWS), image_emb, text_emb)
    return pl.pallas_call(
        project, out_shape=(grad, grad), in_specs=[hbm] * 4, out_specs=(hbm, hbm),
        scratch_shapes=[pltpu.VMEM((2, ROWS, D), jnp.float32), rows(2, ROWS, D), pltpu.VMEM((2, ROWS, D), jnp.float32),
                        pltpu.SemaphoreType.DMA((3, 2, ROWS // PROJECT_ROWS))],
        compiler_params=pltpu.CompilerParams(vmem_limit_bytes=VMEM_LIMIT),
        cost_estimate=pl.CostEstimate(flops=16 * ROWS * D, bytes_accessed=20 * ROWS * D, transcendentals=0),
    )(*sums, image_emb, text_emb)


def solution(mesh):
    in_specs = (P("dp", None), P("dp", None), P("dp"), P(), P())
    out_specs = (P("dp", None), P("dp", None))
    return jax.shard_map(
        per_device, mesh=mesh, in_specs=in_specs, out_specs=out_specs, check_vma=False
    )
```

```python
import jax
import jax.numpy as jnp
from jax import lax
from jax.experimental import pallas as pl
from jax.experimental.pallas import tpu as pltpu
from jax.sharding import PartitionSpec as P

MESH = pl.DeviceIdType.MESH
NDEV = 512
ROWS = 256
D = 1152
CHUNKS = 16
SIZE = 2 * ROWS // CHUNKS
HALF = 128
NORM_ROWS = 64
PROJECT_ROWS = 128
VMEM_LIMIT = 56 * 2**20
LEGS = ("near", "fix", "fj", "fk", "A", "B", "sk", "sl", "sm", "C", "D", "part")
NEXT = {"near": ("fj", "fix"), "sk": ("sl",), "fj": ("fk",), "sl": ("sm", "D"), "fk": ("A", "B"), "sm": ("C",)}
DELAY = {"near": 0, "sk": 0, "fj": 3, "sl": 3, "fk": 6, "sm": 6, "A": 9, "B": 9, "C": 9, "D": 9}
ORDER = ("A", "B", "C", "D", "fk", "sm", "fj", "sl", "near", "sk")
FAR_IDS = 7
PART_AT = 0
WORK = {16: ("image", 0), 17: ("far", 0), 19: ("text", 1), 20: ("far", 1), 22: ("far", 2)}


def coords(i):
    return i // 128, (i // 16) % 8, (i // 2) % 8, i % 2


def index(x, y, z, core):
    return (((x + 8) % 4 * 8 + (y + 16) % 8) * 8 + (z + 16) % 8) * 2 + core


def wrap(i):
    return (i + 2 * NDEV) % NDEV


def side(core):
    return 2 * core - 1


def y_steps(z_start, d):
    return d * 5 + (z_start + 3 * d + 8) // 8 - 1


def along_z(i, n):
    x, y, z, core = coords(i)
    return index(x, y, z + n * side(core), core)


def other_z(i, n):
    x, y, z, core = coords(i)
    return index(x, y, z + n * side(core), 1 - core)


def along_y(i, z_start, d, sign):
    x, y, z, core = coords(i)
    return index(x, y + sign * y_steps(z_start, d), z, core)


def f_z_start(i):
    _, _, z, core = coords(i)
    return (z - 3 * side(core) + 16) % 8


def f_y(i, sign):
    return along_y(i, f_z_start(i), side(i % 2), sign)


def f_hold(owner):
    return f_y(along_z(owner, 3), 1)


def f_owner(i):
    return along_z(f_y(i, -1), -3)


def s_y(i, sign):
    return along_y(i, (i // 2) % 8, -side(i % 2), sign)


def s_hold(owner, n):
    return along_z(s_y(owner, 1), -n)


def s_owner(i, n):
    return s_y(along_z(i, n), -1)


def kernel(scale_ref, bias_ref, ids_ref, img_ref, txt_ref, out_img, out_txt, close, fj, sk, sl, far, raw, coeff, ids,
           send_sem, recv_sem, id_sem, own_sem):
    me = lax.axis_index("dp")
    _, _, z, core = coords(me)
    s = side(core)
    barrier = pltpu.get_barrier_semaphore()

    own_copies = [pltpu.make_async_copy(r, raw.at[a], own_sem.at[a]) for a, r in ((0, txt_ref), (1, img_ref))]
    for copy in own_copies:
        copy.start()

    def is_edge(z, core):
        return z == 7 * core

    f_own, s_own2, s_own3 = f_owner(me), s_owner(me, 2), s_owner(me, 3)
    target = {
        "near": other_z(me, 1), "fix": wrap(me - 16 * s), "fj": other_z(me, -2), "fk": f_y(me, 1),
        "A": wrap(f_own + 86 * s), "B": wrap(f_own - 171 * s),
        "sk": s_y(me, 1), "sl": along_z(me, -2), "sm": along_z(me, -1),
        "C": wrap(s_own3 - 86 * s), "D": wrap(s_own2 + 171 * s), "part": wrap(me - s),
    }
    source = {
        "near": other_z(me, 1), "fix": wrap(me + 16 * s), "fj": other_z(me, -2), "fk": f_y(me, -1),
        "A": f_hold(wrap(me - 86 * s)), "B": f_hold(wrap(me - 171 * s)),
        "sk": s_y(me, -1), "sl": along_z(me, 2), "sm": along_z(me, 1),
        "C": s_hold(wrap(me + 86 * s), 3), "D": s_hold(wrap(me + 171 * s), 2), "part": wrap(me - s),
    }
    only = {"fix": is_edge(z, core), "A": target["A"] != me, "C": target["C"] != me}
    passes = {leg: jnp.where(where, 1, 0) for leg, where in only.items()}

    def signal(device):
        pl.semaphore_signal(barrier, inc=1, device_id=(device,), device_id_type=MESH)

    always = [leg for leg in LEGS if leg not in only]
    for leg in always:
        signal(source[leg])
    for leg, where in only.items():
        pl.when(where)(lambda leg=leg: signal(source[leg]))

    for a in range(2):
        own_copies[a].wait()

        def body(i, carry):
            first = pl.multiple_of(i * NORM_ROWS, NORM_ROWS)
            values = raw[a, pl.ds(first, NORM_ROWS)].astype(jnp.float32)
            norms = jnp.sqrt(jnp.sum(values * values, axis=1, keepdims=True) + 1e-6)
            close[0, pl.ds(a * ROWS + first, NORM_ROWS)] = (values * (1.0 / norms)).astype(jnp.bfloat16)
            return carry
        lax.fori_loop(0, ROWS // NORM_ROWS, body, 0)
    ids[0] = jnp.broadcast_to(ids_ref[...], (8, ROWS))

    pl.semaphore_wait(barrier, len(always) + sum(passes.values()))

    _, _, next_z, next_core = coords(target["near"])
    near_slot = 2 + passes["fix"]
    near_slot_there = 2 + jnp.where(is_edge(next_z, next_core), 1, 0)
    f_next, s_next = target["fk"], target["sm"]
    a_there = jnp.where(wrap(f_owner(f_next) + 86 * s) != f_next, 4, 0)
    c_there = jnp.where(wrap(s_owner(s_next, 3) - 86 * s) != s_next, 5, 2)
    a_here, c_here = 4 * passes["A"], 2 + 3 * passes["C"]

    def far_rows(slot, i):
        per = HALF // SIZE
        return far.at[i // per, pl.ds(pl.multiple_of(slot * HALF + i % per * SIZE, SIZE), SIZE)]

    def to(leg, i):
        rows = pl.ds(i * SIZE, SIZE)
        if leg == "near":
            return close.at[near_slot_there, rows]
        if leg == "fix":
            return close.at[2, rows]
        if leg == "part":
            return close.at[1, rows]
        if leg == "fk":
            return far_rows(a_there, i)
        if leg == "sm":
            return far_rows(c_there, i)
        if leg in "ABCD":
            return far_rows("ABCD".index(leg), i)
        return {"fj": fj, "sk": sk, "sl": sl}[leg].at[rows]

    def at(leg, i):
        if leg == "near":
            return close.at[near_slot, pl.ds(i * SIZE, SIZE)]
        if leg == "fk":
            return far_rows(a_here, i)
        if leg == "sm":
            return far_rows(c_here, i)
        return to(leg, i)

    def id_slot_to(leg):
        far_slot = {"fk": a_there, "sm": c_there, "A": 0, "B": 1, "C": 2, "D": 3}
        if leg in far_slot:
            return FAR_IDS + far_slot[leg]
        return {"near": near_slot_there, "fix": 2, "part": 1, "fj": 4, "sk": 5, "sl": 6}[leg]

    def id_slot_at(leg):
        here = {"near": near_slot, "fk": FAR_IDS + a_here, "sm": FAR_IDS + c_here}
        return here[leg] if leg in here else id_slot_to(leg)

    came_by = {out: leg for leg, outs in NEXT.items() for out in outs}

    def remote(leg, i):
        j = LEGS.index(leg)
        return pltpu.make_async_remote_copy(
            src_ref=at(came_by[leg], i) if leg in came_by else close.at[0, pl.ds(i * SIZE, SIZE)],
            dst_ref=to(leg, i), send_sem=send_sem.at[j, i], recv_sem=recv_sem.at[j, i],
            device_id=(target[leg],), device_id_type=MESH)

    def remote_ids(leg):
        j = LEGS.index(leg)
        return pltpu.make_async_remote_copy(
            src_ref=ids.at[id_slot_at(came_by[leg]) if leg in came_by else 0], dst_ref=ids.at[id_slot_to(leg)],
            send_sem=id_sem.at[0, j], recv_sem=id_sem.at[1, j], device_id=(target[leg],), device_id_type=MESH)

    def do(leg, i, what):
        def act():
            if i == 0:
                getattr(remote_ids(leg), what)()
            getattr(remote(leg, i), what)()
        if leg in only:
            pl.when(only[leg])(act)
        else:
            act()

    for i in range(CHUNKS):
        do("near", i, "start")
        do("sk", i, "start")

    scale, bias = scale_ref[0], bias_ref[0]
    diagonal = lax.broadcasted_iota(jnp.int32, (ROWS, ROWS), 0) == lax.broadcasted_iota(jnp.int32, (ROWS, ROWS), 1)
    my_ids = jnp.sum(jnp.where(diagonal, jnp.broadcast_to(ids_ref[...], (ROWS, ROWS)), 0), axis=1, keepdims=True)

    outs = (out_img, out_txt)

    def gain(a, key_rows, key_ids, first=False):
        count = key_rows.shape[0]
        scores = lax.dot_general(close[0, pl.ds((1 - a) * ROWS, ROWS)], key_rows, (((1,), (1,)), ((), ())),
                                 preferred_element_type=jnp.float32)
        positive = (my_ids == key_ids).astype(jnp.float32)
        coeff[:, pl.ds(0, count)] = (scale * (jax.nn.sigmoid(scale * scores + bias) - positive)).astype(jnp.bfloat16)
        term = jnp.dot(coeff[:, pl.ds(0, count)], key_rows, preferred_element_type=jnp.float32)
        if first:
            outs[a][...] = term
        else:
            outs[a][...] += term

    def close_step(a):
        for i in range(a * CHUNKS // 2, (a + 1) * CHUNKS // 2):
            do("fix", i, "wait_recv")
            do("part", i, "wait_recv")
        key_ids = jnp.concatenate([ids[j, pl.ds(0, 1)] for j in range(3)], axis=1)
        gain(a, close[pl.ds(0, 3), pl.ds(a * ROWS, ROWS)].reshape(3 * ROWS, D), key_ids, first=True)

    def far_step(part_of):
        a, half = part_of // 2, part_of % 2
        lanes = pl.ds(half * HALF, HALF)
        key_ids = jnp.concatenate([ids[FAR_IDS + j, pl.ds(0, 1), lanes] for j in range(4)], axis=1)
        gain(a, far[part_of, pl.ds(0, 4 * HALF)], key_ids)

    last = max(DELAY.values())
    for t in range(CHUNKS + last):
        for leg in ORDER:
            i = t - DELAY[leg]
            if 0 <= i < CHUNKS:
                do(leg, i, "wait_recv")
                for out in NEXT.get(leg, ()):
                    do(out, i, "start")
        if 0 <= t - PART_AT < CHUNKS:
            do("part", t - PART_AT, "start")
        if t in WORK:
            kind, which = WORK[t]
            far_step(which) if kind == "far" else close_step(which)
        if 0 <= t - last < CHUNKS - 1:
            for leg in LEGS:
                do(leg, t - last, "wait_send")
    far_step(3)

    for leg in LEGS:
        do(leg, CHUNKS - 1, "wait_send")


def project(grad_img, grad_txt, img, txt, out_img, out_txt, grads, raw, result, sem):
    pieces = [(a, pl.ds(i * PROJECT_ROWS, PROJECT_ROWS), i) for i in range(ROWS // PROJECT_ROWS) for a in range(2)]

    refs = ((grad_img, img, out_img), (grad_txt, txt, out_txt))

    def load_grad(a, rows, i):
        return pltpu.make_async_copy(refs[a][0].at[rows], grads.at[a, rows], sem.at[0, a, i])

    def load_emb(a, rows, i):
        return pltpu.make_async_copy(refs[a][1].at[rows], raw.at[a, rows], sem.at[1, a, i])

    def store(a, rows, i):
        return pltpu.make_async_copy(result.at[a, rows], refs[a][2].at[rows], sem.at[2, a, i])

    for piece in pieces:
        load_grad(*piece).start()
        load_emb(*piece).start()
    for a, rows, i in pieces:
        load_grad(a, rows, i).wait()
        load_emb(a, rows, i).wait()
        values, grad = raw[a, rows].astype(jnp.float32), grads[a, rows]
        inverse = 1.0 / jnp.sqrt(jnp.sum(values * values, axis=1, keepdims=True) + 1e-6)
        along = jnp.sum(values * grad, axis=1, keepdims=True) * (inverse * inverse)
        result[a, rows] = (grad - values * along) * inverse
        store(a, rows, i).start()
    for piece in pieces:
        store(*piece).wait()


def per_device(image_emb, text_emb, pair_id, logit_scale, logit_bias):
    def rows(*shape):
        return pltpu.VMEM(shape, jnp.bfloat16)
    smem, vmem = (pl.BlockSpec(memory_space=m) for m in (pltpu.SMEM, pltpu.VMEM))
    hbm = pl.BlockSpec(memory_space=pltpu.HBM)
    grad = jax.ShapeDtypeStruct((ROWS, D), jnp.float32)
    sums = pl.pallas_call(
        kernel,
        out_shape=(grad, grad),
        in_specs=[smem, smem, vmem, hbm, hbm],
        out_specs=(vmem, vmem),
        scratch_shapes=[
            rows(4, 2 * ROWS, D), *[rows(2 * ROWS, D)] * 3, rows(4, 6 * HALF, D), rows(2, ROWS, D), rows(ROWS, 3 * ROWS),
            pltpu.VMEM((FAR_IDS + 6, 8, ROWS), jnp.int32),
            pltpu.SemaphoreType.DMA((len(LEGS), CHUNKS)), pltpu.SemaphoreType.DMA((len(LEGS), CHUNKS)),
            pltpu.SemaphoreType.DMA((2, len(LEGS))), pltpu.SemaphoreType.DMA((2,)),
        ],
        compiler_params=pltpu.CompilerParams(collective_id=0, has_side_effects=True, vmem_limit_bytes=VMEM_LIMIT),
        cost_estimate=pl.CostEstimate(flops=28 * ROWS * ROWS * D * 2, bytes_accessed=6 * ROWS * D * 4, transcendentals=14 * ROWS * ROWS),
    )(logit_scale, logit_bias, pair_id.reshape(1, ROWS), image_emb, text_emb)
    return pl.pallas_call(
        project, out_shape=(grad, grad), in_specs=[hbm] * 4, out_specs=(hbm, hbm),
        scratch_shapes=[pltpu.VMEM((2, ROWS, D), jnp.float32), rows(2, ROWS, D), pltpu.VMEM((2, ROWS, D), jnp.float32),
                        pltpu.SemaphoreType.DMA((3, 2, ROWS // PROJECT_ROWS))],
        compiler_params=pltpu.CompilerParams(vmem_limit_bytes=VMEM_LIMIT),
        cost_estimate=pl.CostEstimate(flops=16 * ROWS * D, bytes_accessed=20 * ROWS * D, transcendentals=0),
    )(*sums, image_emb, text_emb)


def solution(mesh):
    in_specs = (P("dp", None), P("dp", None), P("dp"), P(), P())
    out_specs = (P("dp", None), P("dp", None))
    return jax.shard_map(
        per_device, mesh=mesh, in_specs=in_specs, out_specs=out_specs, check_vma=False
    )
```
